128 devices in a mesh: segment: 4 (over x), seq: 16 (over z, y), mp: 2 (over core).
Axes of the slice: x: 4, y: 4, z: 4, core: 2. Of those that a mesh axis runs over, the one named last changes fastest.
Arguments:
- video: bfloat16 [3, 1024, 6144], P(None, 'seq', 'mp'), may hold values from -6 to 6
- caption_kv: bfloat16 [4, 768, 2, 3072], P('segment', 'seq', None, 'mp'), may hold values from -6 to 6
- caption_lengths: int32 [3], replicated, may hold values from 1 to 400, 768 in all
- order: int32 [3], replicated, may hold values from 0 to 2, each once
- gains: float32 [4, 6144], P('segment'), may hold values from 0.25 to 1.75
- w_query: bfloat16 [4, 6144, 3072], P('segment', 'seq', 'mp')
- w_out: bfloat16 [4, 3072, 6144], P('segment', None, 'mp'), may hold values from -0.109375 to 0.109375
Outputs:
- section_out: bfloat16 [4, 3, 1024, 6144], P('segment', None, 'seq', 'mp')
The draws below stay inside these ranges and needn't reach their ends.
Inputs may be any that keep to these rules, and one draw needn't show every extreme that they name: `caption_lengths`: caption lengths sum to 768; the largest is exactly 400. `order`: each sample is named by exactly one micro-batch.
All inputs are finite; a program needn't handle non-finite values.
Results may differ from the reference program's by a relative error of at most 0.009.
Values may be sent and summed in bfloat16 or wider, within the bound.
No kernel may reach another device: no remote copies, remote signals or barrier semaphores. Data moves between devices by JAX's collectives and lax.ppermute only.
A program may use at most 128 MiB of HBM per device.

```python
import math
import jax
import jax.numpy as jnp
import numpy as np
from jax import lax

D = 6144
HEADS = 24
HEAD_DIM = 128
HW = 3072
L = 1024
SAMPLES = 3
CAPROWS = 768
CAPMAX = 400


def draw_video(key, part):
    key = jax.random.fold_in(key, 11)
    base = jnp.clip(jax.random.normal(key, (SAMPLES, L, D), jnp.float32), -6.0, 6.0)
    return base.astype(jnp.bfloat16)


def draw_w_query(key, part):
    key = jax.random.fold_in(key, 12)
    base = jax.random.truncated_normal(key, -6.0, 6.0, (4, D, HW), jnp.float32) * D ** (-0.5)
    return base.astype(jnp.bfloat16)


def draw_caption_kv(key, part):
    key = jax.random.fold_in(key, 13)
    base = jnp.clip(jax.random.normal(key, (4, CAPROWS, 2, HW), jnp.float32), -6.0, 6.0)
    return base.astype(jnp.bfloat16)


def shard_levels(key, shape, shards, least, top_value):
    def one(dim, shards_of):
        draws = jax.random.uniform(jax.random.fold_in(jax.random.fold_in(key, 6), dim), (shards_of,), jnp.float32, least / len(shards), top_value / len(shards))
        return jnp.repeat(jnp.exp(draws), shape[dim] // shards_of).reshape((-1,) + (1,) * (len(shape) - dim - 1))

    level = one(*shards[0])
    for cut in shards[1:]:
        level = level * one(*cut)
    return level


def split_up(number_of, total, most, slope):
    weights = [(1 << 20) // math.isqrt(rank ** slope) + 1 for rank in range(2, number_of + 1)]
    rest, holding = total - most - (number_of - 1), [1] * (number_of - 1)
    while rest > 0:
        free = [i for i in range(number_of - 1) if holding[i] < most]
        mass, remaining = sum([weights[i] for i in free]), rest
        for i in free:
            more = min(most - holding[i], max(1, remaining * weights[i] // mass), rest)
            holding[i] = holding[i] + more
            rest = rest - more
    return np.array([most] + holding)


def ragged(stream_key, count, total, bound, skew):
    if count == 2:
        one = jax.random.randint(stream_key, (), max(1, total - bound), min(bound, total - 1) + 1)
        return jnp.stack([one, total - one])
    sizes = jnp.asarray(split_up(count, total, bound, skew), jnp.int32)
    twos = (count - 1) // 2
    source_of, receiver = sizes[1:1 + 2 * twos:2], sizes[2:2 + 2 * twos:2]
    margin = jnp.minimum(source_of - 1, bound - receiver)
    passed = jax.random.randint(jax.random.fold_in(stream_key, 1), (twos,), 0, 1 << 20) % (margin + 1)
    sizes = sizes.at[1:1 + 2 * twos:2].set(source_of - passed).at[2:2 + 2 * twos:2].set(receiver + passed)
    return sizes[jax.random.permutation(jax.random.fold_in(stream_key, 2), count)]


def centred(stream_key, dims, spread, reach, cuts=(), kind=jnp.bfloat16):
    level = shard_levels(stream_key, dims, cuts, -0.22, 0.18) if cuts else 1.0
    values = jax.random.normal(stream_key, dims, jnp.float32) * spread * level
    return jnp.minimum(jnp.maximum(values, -reach), reach).astype(kind)


def setup_inputs(seed: int = 0) -> dict:
    splits = jax.random.split(jax.random.key(seed), 8)
    return {
        "video": draw_video(jax.random.fold_in(splits[7], 71), 0),
        "caption_kv": draw_caption_kv(jax.random.fold_in(splits[7], 71), 0),
        "caption_lengths": ragged(splits[2], SAMPLES, CAPROWS, CAPMAX, 0).astype(jnp.int32),
        "order": jax.random.permutation(splits[3], SAMPLES).astype(jnp.int32),
        "gains": jnp.clip(1.0 + 0.15 * jax.random.normal(splits[4], (4, D), jnp.float32), 0.25, 1.75),
        "w_query": draw_w_query(jax.random.fold_in(splits[7], 71), 0),
        "w_out": centred(splits[6], (4, HW, D), HW ** -0.5, 0.109375, ((0, 4), (2, 2))),
    }


def section(x, gain, w_query, w_out, kv, valid):
    xf = x.astype(jnp.float32)
    meansq = lax.optimization_barrier(jnp.mean(xf * xf, axis=-1, keepdims=True))
    normed = (xf * lax.rsqrt(meansq + 1e-06) * gain).astype(jnp.bfloat16)
    query = jnp.dot(normed, w_query, preferred_element_type=jnp.float32).astype(jnp.bfloat16)
    rows = query.shape[0]
    qheads = query.astype(jnp.float32).reshape(rows, HEADS, HEAD_DIM)
    keys = kv[:, 0, :].astype(jnp.float32).reshape(CAPROWS, HEADS, HEAD_DIM)
    values = kv[:, 1, :].astype(jnp.float32).reshape(CAPROWS, HEADS, HEAD_DIM)
    scores = jnp.einsum('thd,rhd->htr', qheads, keys) * HEAD_DIM ** (-0.5)
    scores = jnp.where(valid[None, None, :], scores, -1e+30)
    top = lax.optimization_barrier(jnp.max(scores, axis=-1, keepdims=True))
    weights = jnp.where(valid[None, None, :], jnp.exp(scores - top), 0.0)
    total = lax.optimization_barrier(jnp.sum(weights, axis=-1))
    acc = jnp.einsum('htr,rhd->htd', weights, values) / total[:, :, None]
    attended = jnp.transpose(acc, (1, 0, 2)).reshape(rows, HEADS * HEAD_DIM).astype(jnp.bfloat16)
    mixed = xf + jnp.dot(attended, w_out, preferred_element_type=jnp.float32)
    return mixed.astype(jnp.bfloat16)

def reference(video, caption_kv, caption_lengths, order, gains, w_query, w_out):
    offsets = (jnp.cumsum(caption_lengths) - caption_lengths).astype(jnp.int32)
    row_index = jnp.arange(CAPROWS, dtype=jnp.int32)
    results = []
    for micro in range(SAMPLES):
        sample = order[micro]
        current = jnp.take(video, sample, axis=0)
        start_row = offsets[sample]
        valid = (row_index >= start_row) & (row_index < start_row + caption_lengths[sample])
        stacked = []
        for segment_index in range(4):
            current = section(current, gains[segment_index], w_query[segment_index], w_out[segment_index], caption_kv[segment_index], valid)
            stacked.append(current)
        results.append(jnp.stack(stacked))
    return jnp.stack(results, axis=1)
```

```python
import jax
import jax.numpy as jnp
from jax import lax
from jax.experimental import pallas as pl
from jax.experimental.pallas import tpu as pltpu
from jax.sharding import PartitionSpec as P

HEAD_DIM = 128
SIDE = 4
WINDOW = 416


def shift(block, dz, dy):
    pairs = [
        (z * SIDE + y, (z + dz) % SIDE * SIDE + (y + dy) % SIDE)
        for z in range(SIDE)
        for y in range(SIDE)
    ]
    return lax.ppermute(block, "seq", pairs)


def ring(block, along):
    step = (lambda v, d: shift(v, d, 0)) if along == "z" else (lambda v, d: shift(v, 0, d))
    half = block.shape[0] // 2
    below = step(block, 1)
    above = step(block, -1)
    far_low = step(below[:half], 1)
    far_high = step(above[half:], -1)
    return below, above, far_low, far_high


def put(buffer, piece, *index):
    index = tuple(index) + (0,) * (buffer.ndim - len(index))
    return lax.dynamic_update_slice(buffer, piece, index)


def line(block, along, at):
    below, above, far_low, far_high = ring(block, along)
    half = block.shape[0] // 2
    slab = jnp.zeros((SIDE,) + block.shape, block.dtype)
    slab = put(slab, block[None], at)
    slab = put(slab, below[None], (at + 3) % SIDE)
    slab = put(slab, above[None], (at + 1) % SIDE)
    slab = put(slab, far_low[None], (at + 2) % SIDE)
    return put(slab, far_high[None], (at + 2) % SIDE, half)


def plane(block, first, z, y, store):
    if first == "y":
        slab, along, at = line(block, "y", y), "z", z
    else:
        slab, along, at = line(block, "z", z), "y", y
    half = SIDE // 2
    below, above, far_low, far_high = ring(slab, along)
    for piece, off, low in (
        (slab, 0, 0),
        (below, 3, 0),
        (above, 1, 0),
        (far_low, 2, 0),
        (far_high, 2, half),
    ):
        place = (at + off) % SIDE
        if first == "y":
            store(piece[None], place, low)
        else:
            store(piece[:, None], low, place)


def attend_kernel(span, x_ref, gain_ref, w_ref, k_ref, v_ref, out_ref, q_ref):
    xf = x_ref[...].astype(jnp.float32)
    scale = lax.rsqrt(jnp.mean(xf * xf, axis=-1, keepdims=True) + 1e-06)
    normed = (xf * scale * gain_ref[...]).astype(jnp.bfloat16)
    width = w_ref.shape[1]
    tile = 256

    @pl.loop(0, width // tile)
    def _(n):
        cols = pl.ds(pl.multiple_of(n * tile, tile), tile)
        q = jnp.dot(normed, w_ref[:, cols], preferred_element_type=jnp.float32)
        q_ref[:, cols] = q.astype(jnp.bfloat16)

    start = span[0]
    stop = start + span[1]
    rows_total = k_ref.shape[0]
    base = jnp.minimum(start // 16 * 16, rows_total - WINDOW)
    base = pl.multiple_of(base, 16)
    row = base + lax.broadcasted_iota(jnp.int32, (1, WINDOW), 1)
    valid = (row >= start) & (row < stop)
    for h in range(width // HEAD_DIM):
        cols = slice(h * HEAD_DIM, (h + 1) * HEAD_DIM)
        keys = k_ref[pl.ds(base, WINDOW), cols]
        values = v_ref[pl.ds(base, WINDOW), cols]
        scores = lax.dot_general(
            q_ref[:, cols], keys, (((1,), (1,)), ((), ())), preferred_element_type=jnp.float32
        ) * HEAD_DIM ** (-0.5)
        scores = jnp.where(valid, scores, -1e30)
        top = jnp.max(scores, axis=-1, keepdims=True)
        weights = jnp.where(valid, jnp.exp(scores - top), 0.0)
        total = jnp.sum(weights, axis=-1, keepdims=True)
        acc = jnp.dot(
            weights.astype(jnp.bfloat16), values, preferred_element_type=jnp.float32
        )
        out_ref[:, cols] = (acc / total).astype(jnp.bfloat16)


def attend(span, x, gain, w, keys, values):
    tokens = x.shape[0]
    vmem = pl.BlockSpec(memory_space=pltpu.VMEM)
    return pl.pallas_call(
        attend_kernel,
        out_shape=jax.ShapeDtypeStruct((tokens, w.shape[1]), jnp.bfloat16),
        in_specs=[pl.BlockSpec(memory_space=pltpu.SMEM)] + [vmem] * 5,
        out_specs=vmem,
        scratch_shapes=[pltpu.VMEM((tokens, w.shape[1]), jnp.bfloat16)],
        compiler_params=pltpu.CompilerParams(vmem_limit_bytes=8 * 1024 * 1024),
        cost_estimate=pl.CostEstimate(
            flops=2 * tokens * w.shape[0] * w.shape[1],
            bytes_accessed=2 * w.shape[0] * w.shape[1],
            transcendentals=0,
        ),
    )(span, x, gain, w, keys, values)


def body(video, caption_kv, caption_lengths, order, gains, w_query, w_out):
    samples = video.shape[0]
    segments = lax.axis_size("segment")
    here = lax.axis_index("segment")
    seq = lax.axis_index("seq")
    z, y = seq // SIDE, seq % SIDE
    w_local = w_query[0]
    depth, width = w_local.shape
    rows = caption_kv.shape[1]
    half = width // 2
    count = SIDE * SIDE

    box = {
        "w": jnp.zeros((SIDE, SIDE, depth, width), jnp.bfloat16),
        "k": jnp.zeros((SIDE, SIDE, rows, width), jnp.bfloat16),
        "v": jnp.zeros((SIDE, SIDE, rows, width), jnp.bfloat16),
    }
    kv_local = jnp.concatenate([caption_kv[0, :, 0, :], caption_kv[0, :, 1, :]], axis=0)
    for part, first in ((0, "y"), (1, "z")):
        column = part * half

        def store_w(piece, zp, yp, column=column):
            box["w"] = put(box["w"], piece, zp, yp, 0, column)

        def store_kv(piece, zp, yp, column=column):
            box["k"] = put(box["k"], piece[:, :, :rows], zp, yp, 0, column)
            box["v"] = put(box["v"], piece[:, :, rows:], zp, yp, 0, column)

        plane(w_local[:, column : column + half], first, z, y, store_w)
        plane(kv_local[:, column : column + half], first, z, y, store_kv)
    w_whole = box["w"].reshape(count * depth, width)
    keys = box["k"].reshape(count * rows, width)
    values = box["v"].reshape(count * rows, width)

    offsets = jnp.cumsum(caption_lengths) - caption_lengths
    out_weight = w_out[0]
    received = jnp.zeros_like(video[0])
    section_out = jnp.zeros_like(video)
    for tick in range(samples + segments - 1):
        micro = tick - here
        active = (micro >= 0) & (micro < samples)
        slot = jnp.clip(micro, 0, samples - 1)
        sample = order[slot]
        first = lax.dynamic_index_in_dim(video, sample, 0, keepdims=False)
        current = jnp.where(here == 0, first, received)
        whole = lax.all_gather(current, "mp", axis=1, tiled=True)
        span = jnp.stack([offsets[sample], caption_lengths[sample]])
        attended = attend(span, whole, gains, w_whole, keys, values)
        projected = jnp.dot(
            lax.all_gather(attended, "mp", axis=1, tiled=True),
            out_weight,
            preferred_element_type=jnp.float32,
        )
        mixed = (current.astype(jnp.float32) + projected).astype(jnp.bfloat16)
        if tick < samples + segments - 2:
            received = lax.ppermute(
                mixed, "segment", [(i, i + 1) for i in range(segments - 1)]
            )
        updated = lax.dynamic_update_index_in_dim(section_out, mixed, slot, 0)
        section_out = jnp.where(active, updated, section_out)
    return section_out[None]


def solution(mesh):
    in_specs = (
        P(None, "seq", "mp"),
        P("segment", "seq", None, "mp"),
        P(),
        P(),
        P("segment", None),
        P("segment", "seq", "mp"),
        P("segment", None, "mp"),
    )
    out_specs = P("segment", None, "seq", "mp")
    return jax.shard_map(body, mesh=mesh, in_specs=in_specs, out_specs=out_specs, check_vma=False)
```

```python
import functools

import jax
import jax.numpy as jnp
from jax import lax
from jax.experimental import pallas as pl
from jax.experimental.pallas import tpu as pltpu
from jax.sharding import PartitionSpec as P

HEAD_DIM = 128
TILE = 256
LONGEST = 400
MIB = 1024 * 1024

SMEM = pl.BlockSpec(memory_space=pltpu.SMEM)
VMEM = pl.BlockSpec(memory_space=pltpu.VMEM)
HBM = pl.BlockSpec(memory_space=pltpu.HBM)


def attend_tile(n, query, valid, keys, values, out_ref):
    heads = range(TILE // HEAD_DIM)
    cols = [slice(n * TILE + h * HEAD_DIM, n * TILE + (h + 1) * HEAD_DIM) for h in heads]
    scores = [
        lax.dot_general(
            query[:, h * HEAD_DIM : (h + 1) * HEAD_DIM],
            keys[:, cols[h]],
            (((1,), (1,)), ((), ())),
            preferred_element_type=jnp.float32,
        )
        * HEAD_DIM ** (-0.5)
        for h in heads
    ]
    scores = [jnp.where(valid, s, -1e30) for s in scores]
    tops = [jnp.max(s, axis=-1, keepdims=True) for s in scores]
    weights = [jnp.where(valid, jnp.exp(s - t), 0.0) for s, t in zip(scores, tops)]
    totals = [jnp.sum(w, axis=-1, keepdims=True) for w in weights]
    sums = [
        jnp.dot(w.astype(jnp.bfloat16), values[:, c], preferred_element_type=jnp.float32)
        for w, c in zip(weights, cols)
    ]
    for c, acc, total in zip(cols, sums, totals):
        out_ref[:, c] = (acc / total).astype(jnp.bfloat16)


def keep_kernel(whole_ref, kept_ref, sems):
    count, blocks, depth, tile = kept_ref.shape
    copies = [
        pltpu.make_async_copy(
            whole_ref.at[:, pl.ds(0, depth), pl.ds(n * tile, tile)], kept_ref.at[n], sems.at[n]
        )
        for n in range(count)
    ]
    for copy in copies:
        copy.start()
    for copy in copies:
        copy.wait()


def keep(whole, depth):
    return pl.pallas_call(
        keep_kernel,
        out_shape=jax.ShapeDtypeStruct((whole.shape[2] // TILE, whole.shape[0], depth, TILE), jnp.bfloat16),
        in_specs=[HBM],
        out_specs=VMEM,
        scratch_shapes=[pltpu.SemaphoreType.DMA((whole.shape[2] // TILE,))],
        compiler_params=pltpu.CompilerParams(vmem_limit_bytes=22 * MIB),
    )(whole)


def attend_kernel(
    lengths, order, slot, x_ref, kept_ref, whole_ref, out_ref, keys, values, kv_sems
):
    tokens, features = x_ref.shape
    tiles, blocks, depth, _ = kept_ref.shape
    rows = keys.shape[1]

    sample = order[slot[0]]
    start = jnp.int32(0)
    for i in range(lengths.shape[0] - 1):
        start = start + jnp.where(i < sample, lengths[i], 0)
    stop = start + lengths[sample]
    first = jnp.minimum(start // rows, blocks - keys.shape[0])
    captions = [
        pltpu.make_async_copy(
            whole_ref.at[pl.ds(first, keys.shape[0]), pl.ds(depth + i * rows, rows)],
            buffer,
            kv_sems.at[i],
        )
        for i, buffer in enumerate((keys, values))
    ]
    for copy in captions:
        copy.start()
    span = keys.shape[0] * rows
    row = first * rows + lax.broadcasted_iota(jnp.int32, (1, span), 1)
    valid = (row >= start) & (row < stop)
    keys_2d = keys.reshape(span, keys.shape[2])
    values_2d = values.reshape(span, values.shape[2])
    chunk = 512
    squares = jnp.zeros((tokens, chunk), jnp.float32)
    for at in range(0, features, chunk):
        xf = x_ref[:, at : at + chunk].astype(jnp.float32)
        squares = squares + xf * xf
    scale = lax.rsqrt(jnp.sum(squares, axis=-1, keepdims=True) / features + 1e-06)
    query = None
    for n in range(tiles):
        if n == 1:
            for copy in captions:
                copy.wait()
        weight = kept_ref[n].reshape(blocks * depth, TILE)
        product = jnp.dot(x_ref[...], weight, preferred_element_type=jnp.float32)
        if n > 0:
            attend_tile(n - 1, query, valid, keys_2d, values_2d, out_ref)
        query = (product * scale).astype(jnp.bfloat16)
    attend_tile(tiles - 1, query, valid, keys_2d, values_2d, out_ref)


def attend(lengths, order, slot, x, kept, whole):
    tokens, features = x.shape
    blocks, block, width = whole.shape
    depth = features // blocks
    rows = (block - depth) // 2
    span = min((LONGEST + rows - 2) // rows + 1, blocks)
    caption = pltpu.VMEM((span, rows, width), jnp.bfloat16)
    return pl.pallas_call(
        attend_kernel,
        out_shape=jax.ShapeDtypeStruct((tokens, width), jnp.bfloat16),
        in_specs=[SMEM] * 3 + [VMEM, VMEM, HBM],
        out_specs=VMEM,
        scratch_shapes=[
            caption,
            caption,
            pltpu.SemaphoreType.DMA((2,)),
        ],
        compiler_params=pltpu.CompilerParams(vmem_limit_bytes=ATTEND_MIB * MIB),
        cost_estimate=pl.CostEstimate(
            flops=2 * tokens * features * width,
            bytes_accessed=2 * features * width,
            transcendentals=0,
        ),
    )(lengths, order, slot, x, kept, whole)


ATTEND_MIB = 14


def project_kernel(column, a_ref, w_ref, x_ref, out_ref):
    tile = 512

    @pl.loop(0, out_ref.shape[1] // tile)
    def _(n):
        cols = pl.ds(pl.multiple_of(n * tile, tile), tile)
        from_cols = pl.ds(pl.multiple_of(column + n * tile, tile), tile)
        p = jnp.dot(a_ref[...], w_ref[:, from_cols], preferred_element_type=jnp.float32)
        out_ref[:, cols] = (x_ref[:, cols].astype(jnp.float32) + p).astype(jnp.bfloat16)


def project(attended, w, x, column):
    return pl.pallas_call(
        functools.partial(project_kernel, column),
        out_shape=jax.ShapeDtypeStruct(x.shape, jnp.bfloat16),
        in_specs=[VMEM] * 3,
        out_specs=VMEM,
        compiler_params=pltpu.CompilerParams(vmem_limit_bytes=22 * MIB),
        cost_estimate=pl.CostEstimate(
            flops=2 * x.shape[0] * w.shape[0] * x.shape[1],
            bytes_accessed=2 * w.shape[0] * x.shape[1],
            transcendentals=0,
        ),
    )(attended, w, x)


def body(video, caption_kv, caption_lengths, order, gains, w_query, w_out):
    samples = video.shape[0]
    segments = lax.axis_size("segment")
    here = lax.axis_index("segment")
    seq = lax.axis_index("seq")
    depth = w_query.shape[1]

    gain = lax.dynamic_slice_in_dim(gains[0], seq * depth, depth)
    weight = (w_query[0].astype(jnp.float32) * gain[:, None]).astype(jnp.bfloat16)
    local = jnp.concatenate(
        [weight, caption_kv[0, :, 0, :], caption_kv[0, :, 1, :]], axis=0
    )
    gathered = lax.all_gather(local, "seq", axis=0)
    kept = keep(gathered, depth)

    out_weight = w_out[0]
    received = None
    results = []
    last = samples + segments - 2
    for tick in range(last + 1):
        slot = jnp.clip(tick - here, 0, samples - 1).astype(jnp.int32)[None]
        if tick < samples:
            current = lax.dynamic_index_in_dim(video, order[tick], 0, keepdims=False)
            if tick:
                current = jnp.where(here == 0, current, received)
        else:
            current = received
        whole = lax.all_gather(current, "mp", axis=1, tiled=True)
        attended = attend(caption_lengths, order, slot, whole, kept, gathered)
        attended = lax.all_gather(attended, "mp", axis=1, tiled=True)
        mixed = project(attended, out_weight, current, 0)
        if tick < last:
            received = lax.ppermute(
                mixed, "segment", [(i, i + 1) for i in range(segments - 1)]
            )
        results.append(mixed)
    stacked = jnp.stack(results)
    return lax.dynamic_slice_in_dim(stacked, here, samples, 0)[None]


def solution(mesh):
    in_specs = (
        P(None, "seq", "mp"),
        P("segment", "seq", None, "mp"),
        P(),
        P(),
        P("segment", None),
        P("segment", "seq", "mp"),
        P("segment", None, "mp"),
    )
    out_specs = P("segment", None, "seq", "mp")
    return jax.shard_map(body, mesh=mesh, in_specs=in_specs, out_specs=out_specs, check_vma=False)
```

```python
import functools

import jax
import jax.numpy as jnp
from jax import lax
from jax.experimental import pallas as pl
from jax.experimental.pallas import tpu as pltpu
from jax.sharding import PartitionSpec as P

HEAD_DIM = 128
TILE = 256
WINDOW = 416
SIDE = 4
MIB = 1024 * 1024

SMEM = pl.BlockSpec(memory_space=pltpu.SMEM)
VMEM = pl.BlockSpec(memory_space=pltpu.VMEM)
HBM = pl.BlockSpec(memory_space=pltpu.HBM)


def attend_tile(n, query, valid, base, k_ref, v_ref, out_ref):
    heads = range(TILE // HEAD_DIM)
    cols = [slice(n * TILE + h * HEAD_DIM, n * TILE + (h + 1) * HEAD_DIM) for h in heads]
    scores = [
        lax.dot_general(
            query[:, h * HEAD_DIM : (h + 1) * HEAD_DIM],
            k_ref[pl.ds(base, WINDOW), cols[h]],
            (((1,), (1,)), ((), ())),
            preferred_element_type=jnp.float32,
        )
        * HEAD_DIM ** (-0.5)
        for h in heads
    ]
    scores = [jnp.where(valid, s, -1e30) for s in scores]
    tops = [jnp.max(s, axis=-1, keepdims=True) for s in scores]
    weights = [jnp.where(valid, jnp.exp(s - t), 0.0) for s, t in zip(scores, tops)]
    totals = [jnp.sum(w, axis=-1, keepdims=True) for w in weights]
    sums = [
        jnp.dot(
            w.astype(jnp.bfloat16),
            v_ref[pl.ds(base, WINDOW), c],
            preferred_element_type=jnp.float32,
        )
        for w, c in zip(weights, cols)
    ]
    for c, acc, total in zip(cols, sums, totals):
        out_ref[:, c] = (acc / total).astype(jnp.bfloat16)


def shift(block, axis, step):
    dz, dy = (step, 0) if axis == "z" else (0, step)
    pairs = [
        (z * SIDE + y, (z + dz) % SIDE * SIDE + (y + dy) % SIDE)
        for z in range(SIDE)
        for y in range(SIDE)
    ]
    return lax.ppermute(block, "seq", pairs)


def ring(block, axis):
    half = block.shape[0] // 2
    below = shift(block, axis, 1)
    above = shift(block, axis, -1)
    return below, above, shift(below[:half], axis, 1), shift(above[half:], axis, -1)


def pack_kernel(axes, place, *refs):
    count = len(axes)
    ins, outs, sems = refs[: 5 * count], refs[5 * count : 6 * count], refs[-1]
    copies = []
    for group, (axis, slab) in enumerate(zip(axes, outs)):
        at = place[0 if axis == "z" else 1]
        own, below, above, low, high = ins[5 * group : 5 * group + 5]
        half = own.shape[0] // 2
        for src, dst in (
            (own, slab.at[at]),
            (below, slab.at[(at + 3) % SIDE]),
            (above, slab.at[(at + 1) % SIDE]),
            (low, slab.at[(at + 2) % SIDE, pl.ds(0, half)]),
            (high, slab.at[(at + 2) % SIDE, pl.ds(half, half)]),
        ):
            copies.append(pltpu.make_async_copy(src, dst, sems.at[len(copies)]))
    for copy in copies:
        copy.start()
    for copy in copies:
        copy.wait()


def pack(place, axes, rings):
    shape = jax.ShapeDtypeStruct((SIDE,) + rings[0][0].shape, jnp.bfloat16)
    return pl.pallas_call(
        functools.partial(pack_kernel, axes),
        out_shape=[shape] * len(axes),
        in_specs=[SMEM] + [HBM] * (5 * len(axes)),
        out_specs=[VMEM] * len(axes),
        scratch_shapes=[pltpu.SemaphoreType.DMA((5 * len(axes),))],
        compiler_params=pltpu.CompilerParams(vmem_limit_bytes=16 * MIB),
    )(place, *[piece for group in rings for piece in group])


def gather(place, blocks):
    firsts = [first for _, first, _ in blocks]
    slabs = pack(place, firsts, [(b,) + ring(b, first) for b, first, _ in blocks])
    pieces = []
    for slab, (_, first, column) in zip(slabs, blocks):
        axis = "z" if first == "y" else "y"
        below, above, low, high = ring(slab, axis)
        pieces += [
            (slab, axis, 0, 0, column),
            (below, axis, 3, 0, column),
            (above, axis, 1, 0, column),
            (low, axis, 2, 0, column),
            (high, axis, 2, SIDE // 2, column),
        ]
    return pieces


def keep_pieces_kernel(plan, place, _, *refs):
    pieces, kept_ref, sems = refs[: len(plan)], refs[-2], refs[-1]
    copies = []
    for ref, (axis, distance, low, column) in zip(pieces, plan):
        run = pl.ds(low, ref.shape[0])
        if axis == "z":
            at = ((place[0] + distance) % SIDE, run)
        else:
            at = (run, (place[1] + distance) % SIDE)
        for n in range(column // TILE, (column + ref.shape[2]) // TILE):
            copies.append(
                pltpu.make_async_copy(
                    ref.at[:, :, pl.ds(n * TILE - column, TILE)],
                    kept_ref.at[(n,) + at],
                    sems.at[len(copies)],
                )
            )
    for copy in copies:
        copy.start()
    for copy in copies:
        copy.wait()


def keep_pieces(place, after, pieces, depth, tiles):
    plan = [entry[1:] for entry in pieces]
    kept = pl.pallas_call(
        functools.partial(keep_pieces_kernel, plan),
        out_shape=jax.ShapeDtypeStruct((tiles, SIDE, SIDE, depth, TILE), jnp.bfloat16),
        in_specs=[SMEM, VMEM] + [HBM] * len(plan),
        out_specs=VMEM,
        scratch_shapes=[pltpu.SemaphoreType.DMA((len(plan) * tiles,))],
        compiler_params=pltpu.CompilerParams(vmem_limit_bytes=PIECES_MIB * MIB),
    )(place, after, *[entry[0] for entry in pieces])
    return kept.reshape(tiles, SIDE * SIDE, depth, TILE)


def keep_kernel(whole_ref, kept_ref, k_ref, v_ref, sems):
    count, blocks, depth, tile = kept_ref.shape
    rows = k_ref.shape[1]
    chunk = whole_ref.shape[2]
    copies = [
        pltpu.make_async_copy(
            whole_ref.at[:, pl.ds(0, depth), pl.ds(n * tile, tile)], kept_ref.at[n], sems.at[n]
        )
        for n in range(count)
    ]
    start = depth
    for target in (k_ref, v_ref):
        for column in range(0, target.shape[2], chunk):
            copies.append(
                pltpu.make_async_copy(
                    whole_ref.at[:, pl.ds(start, rows)],
                    target.at[:, :, pl.ds(column, chunk)],
                    sems.at[len(copies)],
                )
            )
            start += rows
    for copy in copies:
        copy.start()
    for copy in copies:
        copy.wait()


def keep(whole, depth, width):
    blocks, block, chunk = whole.shape
    chunks = width // chunk
    rows = (block - depth) // (2 * chunks)
    caption = jax.ShapeDtypeStruct((blocks, rows, width), jnp.bfloat16)
    kept, keys, values = pl.pallas_call(
        keep_kernel,
        out_shape=[
            jax.ShapeDtypeStruct((chunk // TILE, blocks, depth, TILE), jnp.bfloat16),
            caption,
            caption,
        ],
        in_specs=[HBM],
        out_specs=[VMEM] * 3,
        scratch_shapes=[pltpu.SemaphoreType.DMA((chunk // TILE + 2 * chunks,))],
        compiler_params=pltpu.CompilerParams(vmem_limit_bytes=KEEP_MIB * MIB),
    )(whole)
    return kept, keys.reshape(blocks * rows, width), values.reshape(blocks * rows, width)


def attend_kernel(
    lengths, order, slot, x_ref, ring_ref, kept_ref, k_ref, v_ref, out_ref
):
    tokens, features = x_ref.shape
    blocks, depth = kept_ref.shape[1:3]
    early = ring_ref.shape[0]
    tiles = early + kept_ref.shape[0]
    sample = order[slot[0]]
    start = jnp.int32(0)
    for i in range(lengths.shape[0] - 1):
        start = start + jnp.where(i < sample, lengths[i], 0)
    stop = start + lengths[sample]
    base = pl.multiple_of(jnp.minimum(start // 16 * 16, k_ref.shape[0] - WINDOW), 16)
    row = base + lax.broadcasted_iota(jnp.int32, (1, WINDOW), 1)
    valid = (row >= start) & (row < stop)
    step = 512
    squares = jnp.zeros((tokens, step), jnp.float32)
    for at in range(0, features, step):
        xf = x_ref[:, at : at + step].astype(jnp.float32)
        squares = squares + xf * xf
    scale = lax.rsqrt(jnp.sum(squares, axis=-1, keepdims=True) / features + 1e-06)
    query = None
    for n in range(tiles):
        weight = ring_ref[n] if n < early else kept_ref[n - early]
        weight = weight.reshape(blocks * depth, TILE)
        product = jnp.dot(x_ref[...], weight, preferred_element_type=jnp.float32)
        if n > 0:
            attend_tile(n - 1, query, valid, base, k_ref, v_ref, out_ref)
        query = (product * scale).astype(jnp.bfloat16)
    attend_tile(tiles - 1, query, valid, base, k_ref, v_ref, out_ref)


def attend(lengths, order, slot, x, ring_tiles, kept, keys, values):
    tokens, features = x.shape
    width = keys.shape[1]
    return pl.pallas_call(
        attend_kernel,
        out_shape=jax.ShapeDtypeStruct((tokens, width), jnp.bfloat16),
        in_specs=[SMEM] * 3 + [VMEM] * 5,
        out_specs=VMEM,
        compiler_params=pltpu.CompilerParams(vmem_limit_bytes=ATTEND_MIB * MIB),
        cost_estimate=pl.CostEstimate(
            flops=2 * tokens * features * width,
            bytes_accessed=2 * features * width,
            transcendentals=0,
        ),
    )(lengths, order, slot, x, ring_tiles, kept, keys, values)


ATTEND_MIB = 8
PIECES_MIB = 8
KEEP_MIB = 16


def hold_kernel(src_ref, dst_ref, sem):
    copy = pltpu.make_async_copy(src_ref, dst_ref, sem)
    copy.start()
    copy.wait()


def hold(w):
    return pl.pallas_call(
        hold_kernel,
        out_shape=jax.ShapeDtypeStruct(w.shape, w.dtype),
        in_specs=[HBM],
        out_specs=VMEM,
        scratch_shapes=[pltpu.SemaphoreType.DMA],
        compiler_params=pltpu.CompilerParams(vmem_limit_bytes=1 * MIB),
    )(w)


def project_kernel(column, a_ref, w_ref, x_ref, out_ref):
    tile = 512

    @pl.loop(0, out_ref.shape[1] // tile)
    def _(n):
        cols = pl.ds(pl.multiple_of(n * tile, tile), tile)
        from_cols = pl.ds(pl.multiple_of(column + n * tile, tile), tile)
        p = jnp.dot(a_ref[...], w_ref[:, from_cols], preferred_element_type=jnp.float32)
        out_ref[:, cols] = (x_ref[:, cols].astype(jnp.float32) + p).astype(jnp.bfloat16)


def project(attended, w, x, column):
    return pl.pallas_call(
        functools.partial(project_kernel, column),
        out_shape=jax.ShapeDtypeStruct(x.shape, jnp.bfloat16),
        in_specs=[VMEM] * 3,
        out_specs=VMEM,
        compiler_params=pltpu.CompilerParams(vmem_limit_bytes=4 * MIB),
        cost_estimate=pl.CostEstimate(
            flops=2 * x.shape[0] * w.shape[0] * x.shape[1],
            bytes_accessed=2 * w.shape[0] * x.shape[1],
            transcendentals=0,
        ),
    )(attended, w, x)


def body(video, caption_kv, caption_lengths, order, gains, w_query, w_out):
    samples = video.shape[0]
    segments = lax.axis_size("segment")
    here = lax.axis_index("segment")
    seq = lax.axis_index("seq")
    depth, width = w_query.shape[1:]

    gain = lax.dynamic_slice_in_dim(gains[0], seq * depth, depth)
    weight = (w_query[0].astype(jnp.float32) * gain[:, None]).astype(jnp.bfloat16)
    third = width // 3
    early = width - third
    captions = [
        caption_kv[0, :, i, c : c + third] for i in range(2) for c in range(0, width, third)
    ]
    local = jnp.concatenate([weight[:, early:]] + captions, axis=0)
    gathered = lax.all_gather(local, "seq", axis=0)
    place = jnp.stack([seq // SIDE, seq % SIDE]).astype(jnp.int32)
    blocks = [(weight[:, : early // 2], "y", 0), (weight[:, early // 2 : early], "z", early // 2)]
    kept, keys, values = keep(gathered, depth, width)
    ring_tiles = keep_pieces(place, kept, gather(place, blocks), depth, early // TILE)

    out_weight = hold(w_out[0])
    received = None
    results = []
    last = samples + segments - 2
    for tick in range(last + 1):
        slot = jnp.clip(tick - here, 0, samples - 1).astype(jnp.int32)[None]
        if tick < samples:
            current = lax.dynamic_index_in_dim(video, order[tick], 0, keepdims=False)
            if tick:
                current = jnp.where(here == 0, current, received)
        else:
            current = received
        whole = lax.all_gather(current, "mp", axis=1, tiled=True)
        attended = attend(caption_lengths, order, slot, whole, ring_tiles, kept, keys, values)
        attended = lax.all_gather(attended, "mp", axis=1, tiled=True)
        mixed = project(attended, out_weight, current, 0)
        if tick < last:
            received = lax.ppermute(
                mixed, "segment", [(i, i + 1) for i in range(segments - 1)]
            )
        results.append(mixed)
    stacked = jnp.stack(results)
    return lax.dynamic_slice_in_dim(stacked, here, samples, 0)[None]


def solution(mesh):
    in_specs = (
        P(None, "seq", "mp"),
        P("segment", "seq", None, "mp"),
        P(),
        P(),
        P("segment", None),
        P("segment", "seq", "mp"),
        P("segment", None, "mp"),
    )
    out_specs = P("segment", None, "seq", "mp")
    return jax.shard_map(body, mesh=mesh, in_specs=in_specs, out_specs=out_specs, check_vma=False)
```

```python
import functools

import jax
import jax.numpy as jnp
from jax import lax
from jax.experimental import pallas as pl
from jax.experimental.pallas import tpu as pltpu
from jax.sharding import PartitionSpec as P

HEAD_DIM = 128
TILE = 256
WINDOW = 416
SIDE = 4
MIB = 1024 * 1024

SMEM = pl.BlockSpec(memory_space=pltpu.SMEM)
VMEM = pl.BlockSpec(memory_space=pltpu.VMEM)
HBM = pl.BlockSpec(memory_space=pltpu.HBM)


def attend_tile(n, query, valid, base, k_ref, v_ref, out_ref):
    heads = range(TILE // HEAD_DIM)
    cols = [slice(n * TILE + h * HEAD_DIM, n * TILE + (h + 1) * HEAD_DIM) for h in heads]
    scores = [
        lax.dot_general(
            query[:, h * HEAD_DIM : (h + 1) * HEAD_DIM],
            k_ref[pl.ds(base, WINDOW), cols[h]],
            (((1,), (1,)), ((), ())),
            preferred_element_type=jnp.float32,
        )
        * HEAD_DIM ** (-0.5)
        for h in heads
    ]
    scores = [jnp.where(valid, s, -1e30) for s in scores]
    tops = [jnp.max(s, axis=-1, keepdims=True) for s in scores]
    weights = [jnp.where(valid, jnp.exp(s - t), 0.0) for s, t in zip(scores, tops)]
    totals = [jnp.sum(w, axis=-1, keepdims=True) for w in weights]
    sums = [
        jnp.dot(
            w.astype(jnp.bfloat16),
            v_ref[pl.ds(base, WINDOW), c],
            preferred_element_type=jnp.float32,
        )
        for w, c in zip(weights, cols)
    ]
    for c, acc, total in zip(cols, sums, totals):
        out_ref[:, c] = (acc / total).astype(jnp.bfloat16)


def shift(block, axis, step):
    dz, dy = (step, 0) if axis == "z" else (0, step)
    pairs = [
        (z * SIDE + y, (z + dz) % SIDE * SIDE + (y + dy) % SIDE)
        for z in range(SIDE)
        for y in range(SIDE)
    ]
    return lax.ppermute(block, "seq", pairs)


def ring(block, axis):
    half = block.shape[0] // 2
    below = shift(block, axis, 1)
    above = shift(block, axis, -1)
    return below, above, shift(below[:half], axis, 1), shift(above[half:], axis, -1)


def short_ring(block, axis):
    below = shift(block, axis, 1)
    above = shift(block, axis, -1)
    far = shift(below, axis, 1) if axis == "y" else shift(above, axis, -1)
    return below, above, far


def pack_kernel(axes, place, *refs):
    count = len(axes)
    ins, outs, sems = refs[: 4 * count], refs[4 * count : 5 * count], refs[-1]
    copies = []
    for group, (axis, slab) in enumerate(zip(axes, outs)):
        at = place[0 if axis == "z" else 1]
        own, below, above, far = ins[4 * group : 4 * group + 4]
        for src, dst in (
            (own, slab.at[at]),
            (below, slab.at[(at + 3) % SIDE]),
            (above, slab.at[(at + 1) % SIDE]),
            (far, slab.at[(at + 2) % SIDE]),
        ):
            copies.append(pltpu.make_async_copy(src, dst, sems.at[len(copies)]))
    for copy in copies:
        copy.start()
    for copy in copies:
        copy.wait()


def pack(place, axes, rings):
    shape = jax.ShapeDtypeStruct((SIDE,) + rings[0][0].shape, jnp.bfloat16)
    return pl.pallas_call(
        functools.partial(pack_kernel, axes),
        out_shape=[shape] * len(axes),
        in_specs=[SMEM] + [HBM] * (4 * len(axes)),
        out_specs=[VMEM] * len(axes),
        scratch_shapes=[pltpu.SemaphoreType.DMA((4 * len(axes),))],
        compiler_params=pltpu.CompilerParams(vmem_limit_bytes=16 * MIB),
    )(place, *[piece for group in rings for piece in group])


def gather(place, blocks):
    firsts = [first for _, first, _ in blocks]
    slabs = pack(place, firsts, [(b,) + short_ring(b, first) for b, first, _ in blocks])
    pieces = []
    for slab, (_, first, column) in zip(slabs, blocks):
        axis = "z" if first == "y" else "y"
        below, above, low, high = ring(slab, axis)
        pieces += [
            (slab, axis, 0, 0, column),
            (below, axis, 3, 0, column),
            (above, axis, 1, 0, column),
            (low, axis, 2, 0, column),
            (high, axis, 2, SIDE // 2, column),
        ]
    return pieces


def keep_pieces_kernel(plan, place, _, *refs):
    pieces, kept_ref, sems = refs[: len(plan)], refs[-2], refs[-1]
    copies = []
    for ref, (axis, distance, low, column) in zip(pieces, plan):
        run = pl.ds(low, ref.shape[0])
        if axis == "z":
            at = ((place[0] + distance) % SIDE, run)
        else:
            at = (run, (place[1] + distance) % SIDE)
        for n in range(column // TILE, (column + ref.shape[2]) // TILE):
            copies.append(
                pltpu.make_async_copy(
                    ref.at[:, :, pl.ds(n * TILE - column, TILE)],
                    kept_ref.at[(n,) + at],
                    sems.at[len(copies)],
                )
            )
    for copy in copies:
        copy.start()
    for copy in copies:
        copy.wait()


def keep_pieces(place, after, pieces, depth, tiles):
    plan = [entry[1:] for entry in pieces]
    kept = pl.pallas_call(
        functools.partial(keep_pieces_kernel, plan),
        out_shape=jax.ShapeDtypeStruct((tiles, SIDE, SIDE, depth, TILE), jnp.bfloat16),
        in_specs=[SMEM, VMEM] + [HBM] * len(plan),
        out_specs=VMEM,
        scratch_shapes=[pltpu.SemaphoreType.DMA((len(plan) * tiles,))],
        compiler_params=pltpu.CompilerParams(vmem_limit_bytes=PIECES_MIB * MIB),
    )(place, after, *[entry[0] for entry in pieces])
    return kept.reshape(tiles, SIDE * SIDE, depth, TILE)


def keep_kernel(whole_ref, kept_ref, k_ref, v_ref, sems):
    count, blocks, depth, tile = kept_ref.shape
    rows = k_ref.shape[1]
    chunk = whole_ref.shape[2]
    copies = [
        pltpu.make_async_copy(
            whole_ref.at[:, pl.ds(0, depth), pl.ds(n * tile, tile)], kept_ref.at[n], sems.at[n]
        )
        for n in range(count)
    ]
    start = depth
    for target in (k_ref, v_ref):
        for column in range(0, target.shape[2], chunk):
            copies.append(
                pltpu.make_async_copy(
                    whole_ref.at[:, pl.ds(start, rows)],
                    target.at[:, :, pl.ds(column, chunk)],
                    sems.at[len(copies)],
                )
            )
            start += rows
    for copy in copies:
        copy.start()
    for copy in copies:
        copy.wait()


def keep(whole, depth, width):
    blocks, block, chunk = whole.shape
    chunks = width // chunk
    rows = (block - depth) // (2 * chunks)
    caption = jax.ShapeDtypeStruct((blocks, rows, width), jnp.bfloat16)
    kept, keys, values = pl.pallas_call(
        keep_kernel,
        out_shape=[
            jax.ShapeDtypeStruct((chunk // TILE, blocks, depth, TILE), jnp.bfloat16),
            caption,
            caption,
        ],
        in_specs=[HBM],
        out_specs=[VMEM] * 3,
        scratch_shapes=[pltpu.SemaphoreType.DMA((chunk // TILE + 2 * chunks,))],
        compiler_params=pltpu.CompilerParams(vmem_limit_bytes=KEEP_MIB * MIB),
    )(whole)
    return kept, keys.reshape(blocks * rows, width), values.reshape(blocks * rows, width)


def attend_kernel(
    lengths, order, slot, x_ref, ring_ref, kept_ref, k_ref, v_ref, out_ref
):
    tokens, features = x_ref.shape
    blocks, depth = kept_ref.shape[1:3]
    early = ring_ref.shape[0]
    tiles = early + kept_ref.shape[0]
    sample = order[slot[0]]
    start = jnp.int32(0)
    for i in range(lengths.shape[0] - 1):
        start = start + jnp.where(i < sample, lengths[i], 0)
    stop = start + lengths[sample]
    base = pl.multiple_of(jnp.minimum(start // 16 * 16, k_ref.shape[0] - WINDOW), 16)
    row = base + lax.broadcasted_iota(jnp.int32, (1, WINDOW), 1)
    valid = (row >= start) & (row < stop)
    step = 512
    squares = jnp.zeros((tokens, step), jnp.float32)
    for at in range(0, features, step):
        xf = x_ref[:, at : at + step].astype(jnp.float32)
        squares = squares + xf * xf
    scale = lax.rsqrt(jnp.sum(squares, axis=-1, keepdims=True) / features + 1e-06)
    query = None
    for n in range(tiles):
        weight = ring_ref[n] if n < early else kept_ref[n - early]
        weight = weight.reshape(blocks * depth, TILE)
        product = jnp.dot(x_ref[...], weight, preferred_element_type=jnp.float32)
        if n > 0:
            attend_tile(n - 1, query, valid, base, k_ref, v_ref, out_ref)
        query = (product * scale).astype(jnp.bfloat16)
    attend_tile(tiles - 1, query, valid, base, k_ref, v_ref, out_ref)


def attend(lengths, order, slot, x, ring_tiles, kept, keys, values):
    tokens, features = x.shape
    width = keys.shape[1]
    return pl.pallas_call(
        attend_kernel,
        out_shape=jax.ShapeDtypeStruct((tokens, width), jnp.bfloat16),
        in_specs=[SMEM] * 3 + [VMEM] * 5,
        out_specs=VMEM,
        compiler_params=pltpu.CompilerParams(vmem_limit_bytes=ATTEND_MIB * MIB),
        cost_estimate=pl.CostEstimate(
            flops=2 * tokens * features * width,
            bytes_accessed=2 * features * width,
            transcendentals=0,
        ),
    )(lengths, order, slot, x, ring_tiles, kept, keys, values)


ATTEND_MIB = 8
PIECES_MIB = 8
KEEP_MIB = 16


def hold_kernel(src_ref, dst_ref, sem):
    copy = pltpu.make_async_copy(src_ref, dst_ref, sem)
    copy.start()
    copy.wait()


def hold(w):
    return pl.pallas_call(
        hold_kernel,
        out_shape=jax.ShapeDtypeStruct(w.shape, w.dtype),
        in_specs=[HBM],
        out_specs=VMEM,
        scratch_shapes=[pltpu.SemaphoreType.DMA],
        compiler_params=pltpu.CompilerParams(vmem_limit_bytes=1 * MIB),
    )(w)


def project_kernel(column, a_ref, w_ref, x_ref, out_ref):
    tile = 512

    @pl.loop(0, out_ref.shape[1] // tile)
    def _(n):
        cols = pl.ds(pl.multiple_of(n * tile, tile), tile)
        from_cols = pl.ds(pl.multiple_of(column + n * tile, tile), tile)
        p = jnp.dot(a_ref[...], w_ref[:, from_cols], preferred_element_type=jnp.float32)
        out_ref[:, cols] = (x_ref[:, cols].astype(jnp.float32) + p).astype(jnp.bfloat16)


def project(attended, w, x, column):
    return pl.pallas_call(
        functools.partial(project_kernel, column),
        out_shape=jax.ShapeDtypeStruct(x.shape, jnp.bfloat16),
        in_specs=[VMEM] * 3,
        out_specs=VMEM,
        compiler_params=pltpu.CompilerParams(vmem_limit_bytes=4 * MIB),
        cost_estimate=pl.CostEstimate(
            flops=2 * x.shape[0] * w.shape[0] * x.shape[1],
            bytes_accessed=2 * w.shape[0] * x.shape[1],
            transcendentals=0,
        ),
    )(attended, w, x)


def body(video, caption_kv, caption_lengths, order, gains, w_query, w_out):
    samples = video.shape[0]
    segments = lax.axis_size("segment")
    here = lax.axis_index("segment")
    seq = lax.axis_index("seq")
    depth, width = w_query.shape[1:]

    gain = lax.dynamic_slice_in_dim(gains[0], seq * depth, depth)
    weight = (w_query[0].astype(jnp.float32) * gain[:, None]).astype(jnp.bfloat16)
    third = width // 3
    early = width - third
    captions = [
        caption_kv[0, :, i, c : c + third] for i in range(2) for c in range(0, width, third)
    ]
    local = jnp.concatenate([weight[:, early:]] + captions, axis=0)
    gathered = lax.all_gather(local, "seq", axis=0)
    place = jnp.stack([seq // SIDE, seq % SIDE]).astype(jnp.int32)
    blocks = [(weight[:, : early // 2], "y", 0), (weight[:, early // 2 : early], "z", early // 2)]
    kept, keys, values = keep(gathered, depth, width)
    ring_tiles = keep_pieces(place, kept, gather(place, blocks), depth, early // TILE)

    out_weight = hold(w_out[0])
    received = None
    results = []
    last = samples + segments - 2
    for tick in range(last + 1):
        slot = jnp.clip(tick - here, 0, samples - 1).astype(jnp.int32)[None]
        if tick < samples:
            current = lax.dynamic_index_in_dim(video, order[tick], 0, keepdims=False)
            if tick:
                current = jnp.where(here == 0, current, received)
        else:
            current = received
        whole = lax.all_gather(current, "mp", axis=1, tiled=True)
        attended = attend(caption_lengths, order, slot, whole, ring_tiles, kept, keys, values)
        attended = lax.all_gather(attended, "mp", axis=1, tiled=True)
        mixed = project(attended, out_weight, current, 0)
        if tick < last:
            received = lax.ppermute(
                mixed, "segment", [(i, i + 1) for i in range(segments - 1)]
            )
        results.append(mixed)
    stacked = jnp.stack(results)
    return lax.dynamic_slice_in_dim(stacked, here, samples, 0)[None]


def solution(mesh):
    in_specs = (
        P(None, "seq", "mp"),
        P("segment", "seq", None, "mp"),
        P(),
        P(),
        P("segment", None),
        P("segment", "seq", "mp"),
        P("segment", None, "mp"),
    )
    out_specs = P("segment", None, "seq", "mp")
    return jax.shard_map(body, mesh=mesh, in_specs=in_specs, out_specs=out_specs, check_vma=False)
```
